128 devices in a mesh: dp: 4 (over y), ctx: 32 (over z, x, core).
Axes of the slice: x: 4, y: 4, z: 4, core: 2. Of those that a mesh axis runs over, the one named last changes fastest.
Arguments:
- queries: bfloat16 [16384, 64, 128], P(('dp', 'ctx')), parts along dimension 0, may hold values from -6 to 6
- keys: bfloat16 [16384, 8, 128], P(('dp', 'ctx')), parts along dimension 0, may hold values from -6 to 6
- values: bfloat16 [16384, 8, 128], P(('dp', 'ctx')), parts along dimension 0, may hold values from -6 to 6
- output: bfloat16 [16384, 64, 128], P(('dp', 'ctx')), parts along dimension 0, may hold values from -6 to 6
- output_cotangent: bfloat16 [16384, 64, 128], P(('dp', 'ctx')), parts along dimension 0, may hold values from -6 to 6
- logsumexp_rows: float32 [16384, 64], P(('dp', 'ctx')), parts along dimension 0, may hold values from 2 to 4
- doc_lengths: int32 [64], P('dp'), parts along dimension 0, may hold values from 1 to 512, 4096 in all
Outputs:
- query_grad: bfloat16 [16384, 64, 128], P(('dp', 'ctx')), parts along dimension 0
- key_grad: bfloat16 [16384, 8, 128], P(('dp', 'ctx')), parts along dimension 0
- value_grad: bfloat16 [16384, 8, 128], P(('dp', 'ctx')), parts along dimension 0
The draws below stay inside these ranges and needn't reach their ends.
There are 4 independent parts, one for each index of `dp`. The reference program is written for one: setup_inputs(seed, part) draws one part's arguments, and reference() takes and returns one part's arrays. A program takes and returns all parts, laid end to end along the dimension named above; each array names one. Nothing has to cross between parts.
Inputs may be any that keep to these rules, and one draw needn't show every extreme that they name: `doc_lengths`: the 16 lengths sum to 4096; the largest is exactly 512.
All inputs are finite; a program needn't handle non-finite values.
Results may differ from the reference program's by a relative error of at most 0.0057.
Values may be sent and summed in bfloat16 or wider, within the bound.
No kernel may reach another device: no remote copies, remote signals or barrier semaphores. Data moves between devices by JAX's collectives and lax.ppermute only.
A program may use at most 128 MiB of HBM per device.

```python
import math
import jax
import jax.numpy as jnp
import numpy as np
from jax import lax

QUERY_HEADS = 64
KEY_VALUE_HEADS = 8
HEAD_DIM = 128
BLOCK = 512
DOC_MAX = 512
WINDOW_TOKENS = 4096
NDOC = 16


def steps_of(key, extent, shards, smallest, high):
    def one(axis_at, parts):
        draws = jax.random.uniform(jax.random.fold_in(jax.random.fold_in(key, 6), axis_at), (parts,), jnp.float32, smallest / len(shards), high / len(shards))
        return jnp.repeat(jnp.exp(draws), extent[axis_at] // parts).reshape((-1,) + (1,) * (len(extent) - axis_at - 1))

    factor_of = one(*shards[0])
    for cut in shards[1:]:
        factor_of = factor_of * one(*cut)
    return factor_of


def length_profile(count, total, limit, skew):
    weights = [(1 << 20) // math.isqrt(standing ** skew) + 1 for standing in range(2, count + 1)]
    spare, given = total - limit - (count - 1), [1] * (count - 1)
    while spare > 0:
        free = [i for i in range(count - 1) if given[i] < limit]
        mass, left = sum([weights[i] for i in free]), spare
        for i in free:
            addition = min(limit - given[i], max(1, left * weights[i] // mass), spare)
            given[i] = given[i] + addition
            spare = spare - addition
    return np.array([limit] + given)


def uneven(key, amount, total, limit, slope):
    if amount == 2:
        one = jax.random.randint(key, (), max(1, total - limit), min(limit, total - 1) + 1)
        return jnp.stack([one, total - one])
    tallies = jnp.asarray(length_profile(amount, total, limit, slope), jnp.int32)
    couples = (amount - 1) // 2
    source_of, receiver = tallies[1:1 + 2 * couples:2], tallies[2:2 + 2 * couples:2]
    slack = jnp.minimum(source_of - 1, limit - receiver)
    shifted = jax.random.randint(jax.random.fold_in(key, 1), (couples,), 0, 1 << 20) % (slack + 1)
    tallies = tallies.at[1:1 + 2 * couples:2].set(source_of - shifted).at[2:2 + 2 * couples:2].set(receiver + shifted)
    return tallies[jax.random.permutation(jax.random.fold_in(key, 2), amount)]


def centred(own_key, extent, deviation, reach, pieces=(), kind=jnp.bfloat16):
    values = deviation * jax.random.normal(own_key, extent, jnp.float32)
    if pieces:
        values = values * steps_of(own_key, extent, pieces, -0.22, 0.18)
    return jnp.clip(values, -reach, reach).astype(kind)


def setup_inputs(seed: int = 0, part: int = 0) -> dict:
    splits = jax.random.split(jax.random.key(seed), 8)
    part_keys = jax.random.split(jax.random.fold_in(splits[7], part), 8)
    queries = centred(part_keys[0], (WINDOW_TOKENS, QUERY_HEADS, HEAD_DIM), 1.0, 6.0, ((0, 32),))
    keys = centred(part_keys[1], (WINDOW_TOKENS, KEY_VALUE_HEADS, HEAD_DIM), 1.0, 6.0, ((0, 32),))
    values = centred(part_keys[2], (WINDOW_TOKENS, KEY_VALUE_HEADS, HEAD_DIM), 1.0, 6.0, ((0, 32),))
    output = centred(part_keys[3], (WINDOW_TOKENS, QUERY_HEADS, HEAD_DIM), 1.0, 6.0, ((0, 32),))
    output_cotangent = centred(part_keys[4], (WINDOW_TOKENS, QUERY_HEADS, HEAD_DIM), 1.0, 6.0, ((0, 32),))
    logsumexp_rows = jnp.clip(2.0 + 2.0 * jax.random.uniform(part_keys[5], (WINDOW_TOKENS, QUERY_HEADS), jnp.float32) ** steps_of(part_keys[5], (WINDOW_TOKENS, QUERY_HEADS), ((0, 32),), -0.2, 0.2), 2.0, 4.0)
    doc_lengths = uneven(part_keys[6], NDOC, WINDOW_TOKENS, DOC_MAX, 2).astype(jnp.int32)
    return {"queries": queries, "keys": keys, "values": values, "output": output, "output_cotangent": output_cotangent, "logsumexp_rows": logsumexp_rows, "doc_lengths": doc_lengths}


def document_ids(doc_lengths, grand_total):
    ends = jnp.cumsum(doc_lengths).astype(jnp.int32)
    positions = jnp.arange(grand_total, dtype=jnp.int32)
    return jnp.sum((positions[:, None] >= ends[None, :]).astype(jnp.int32), axis=1).astype(jnp.int32)


def group_grads(queries, output_cotangent, logsumexp_rows, output_dot_grad, keys, values, doc_id, block, doc_max):
    grand_total, heads, width = queries.shape
    scale = width ** -0.5
    window = doc_max + block
    key_pad = jnp.concatenate([jnp.zeros((doc_max, width), keys.dtype), keys], 0)
    value_pad = jnp.concatenate([jnp.zeros((doc_max, width), values.dtype), values], 0)
    id_pad = jnp.concatenate([jnp.full((doc_max,), -1, jnp.int32), doc_id], 0)

    def step(carry, index):
        key_acc, value_acc = carry
        start = (index * block).astype(jnp.int32)
        q_blk = lax.dynamic_slice_in_dim(queries, start, block, 0).astype(jnp.float32)
        g_blk = lax.dynamic_slice_in_dim(output_cotangent, start, block, 0).astype(jnp.float32)
        lse_blk = lax.dynamic_slice_in_dim(logsumexp_rows, start, block, 0)
        del_blk = lax.dynamic_slice_in_dim(output_dot_grad, start, block, 0)
        k_win = lax.dynamic_slice_in_dim(key_pad, start, window, 0).astype(jnp.float32)
        v_win = lax.dynamic_slice_in_dim(value_pad, start, window, 0).astype(jnp.float32)
        id_q = lax.dynamic_slice_in_dim(doc_id, start, block, 0)
        id_k = lax.dynamic_slice_in_dim(id_pad, start, window, 0)
        q_pos = start + jnp.arange(block, dtype=jnp.int32)
        k_pos = start - doc_max + jnp.arange(window, dtype=jnp.int32)
        visible = (id_q[:, None] == id_k[None, :]) & (k_pos[None, :] <= q_pos[:, None])
        score = jnp.einsum('qhd,kd->hqk', q_blk, k_win) * scale
        prob = jnp.where(visible[None], jnp.exp(score - lse_blk.T[:, :, None]), 0.0)
        prob_b = prob.astype(jnp.bfloat16).astype(jnp.float32)
        value_part = jnp.einsum('hqk,qhd->kd', prob_b, g_blk)
        dprob = jnp.einsum('qhd,kd->hqk', g_blk, v_win)
        dscore = (prob * (dprob - del_blk.T[:, :, None])).astype(jnp.bfloat16).astype(jnp.float32)
        q_grad = (jnp.einsum('hqk,kd->qhd', dscore, k_win) * scale).astype(jnp.bfloat16)
        key_part = jnp.einsum('hqk,qhd->kd', dscore, q_blk) * scale
        key_acc = lax.dynamic_update_slice_in_dim(key_acc, lax.dynamic_slice_in_dim(key_acc, start, window, 0) + key_part, start, 0)
        value_acc = lax.dynamic_update_slice_in_dim(value_acc, lax.dynamic_slice_in_dim(value_acc, start, window, 0) + value_part, start, 0)
        return (key_acc, value_acc), q_grad

    zeros = jnp.zeros((doc_max + grand_total, width), jnp.float32)
    (key_acc, value_acc), q_grads = lax.scan(step, (zeros, zeros), jnp.arange(grand_total // block, dtype=jnp.int32))
    return q_grads.reshape(grand_total, heads, width), key_acc[doc_max:], value_acc[doc_max:]


def reference(queries, keys, values, output, output_cotangent, logsumexp_rows, doc_lengths):
    grand_total = queries.shape[0]
    heads_per_group = QUERY_HEADS // KEY_VALUE_HEADS
    doc_id = document_ids(doc_lengths, grand_total)
    output_dot_grad = jnp.sum(output_cotangent.astype(jnp.float32) * output.astype(jnp.float32), axis=-1)
    query_by_group = queries.reshape(grand_total, KEY_VALUE_HEADS, heads_per_group, HEAD_DIM).transpose(1, 0, 2, 3)
    grad_by_group = output_cotangent.reshape(grand_total, KEY_VALUE_HEADS, heads_per_group, HEAD_DIM).transpose(1, 0, 2, 3)
    logsumexp_by_group = logsumexp_rows.reshape(grand_total, KEY_VALUE_HEADS, heads_per_group).transpose(1, 0, 2)
    delta_by_group = output_dot_grad.reshape(grand_total, KEY_VALUE_HEADS, heads_per_group).transpose(1, 0, 2)
    k_groups = keys.transpose(1, 0, 2)
    v_groups = values.transpose(1, 0, 2)

    def one_group(items):
        q_g, g_g, lse_g, del_g, k_g, v_g = items
        return group_grads(q_g, g_g, lse_g, del_g, k_g, v_g, doc_id, BLOCK, DOC_MAX)

    q_grad, k_grad, v_grad = lax.map(one_group, (query_by_group, grad_by_group, logsumexp_by_group, delta_by_group, k_groups, v_groups))
    query_grad = q_grad.transpose(1, 0, 2, 3).reshape(grand_total, QUERY_HEADS, HEAD_DIM)
    key_grad = k_grad.transpose(1, 0, 2).astype(jnp.bfloat16)
    value_grad = v_grad.transpose(1, 0, 2).astype(jnp.bfloat16)
    return query_grad, key_grad, value_grad
```

```python
import functools

import jax
import jax.numpy as jnp
from jax import lax
from jax.experimental import pallas as pl
from jax.experimental.pallas import tpu as pltpu
from jax.sharding import PartitionSpec as P

TOK = 128
WIDTH = 128
HEADS = 64
KV = 8
HALF = KV // 2
ROWS = TOK * (HEADS // KV)
NDOC = 16
SCALE = WIDTH ** (-0.5)
LOG2E = 1.4426950408889634
F32 = jnp.float32
BF16 = jnp.bfloat16
VMEM_LIMIT = 48 * 1024 * 1024


def params(limit=VMEM_LIMIT):
    return pltpu.CompilerParams(vmem_limit_bytes=limit)


def dot(a, b, ca, cb):
    return lax.dot_general(a, b, (((ca,), (cb,)), ((), ())), preferred_element_type=F32)


def kv_prep_kernel(where, k_ref, v_ref, same_ref, flip_ref, scr):
    core = where[0] % 2
    k_t = jnp.transpose(k_ref[...].astype(F32), (1, 0, 2)).astype(BF16)
    v_t = jnp.transpose(v_ref[...].astype(F32), (1, 0, 2)).astype(BF16)
    for half in range(2):
        scr[half, :HALF] = k_t[half * HALF : (half + 1) * HALF]
        scr[half, HALF:] = v_t[half * HALF : (half + 1) * HALF]
    same_ref[...] = scr[core]
    flip_ref[...] = scr[1 - core]


def kv_prep(where, keys, values):
    half = jax.ShapeDtypeStruct((KV, TOK, WIDTH), BF16)
    return pl.pallas_call(
        kv_prep_kernel,
        out_shape=(half, half),
        in_specs=[
            pl.BlockSpec(memory_space=pltpu.SMEM),
            pl.BlockSpec(memory_space=pltpu.VMEM),
            pl.BlockSpec(memory_space=pltpu.VMEM),
        ],
        out_specs=(pl.BlockSpec(memory_space=pltpu.VMEM),) * 2,
        scratch_shapes=[pltpu.VMEM((2, KV, TOK, WIDTH), BF16)],
        compiler_params=params(),
        name="kv_prep",
    )(where, keys, values)


def delta_kernel(g_ref, o_ref, d_ref):
    prod = g_ref[...].astype(F32) * o_ref[...].astype(F32)
    ones = jnp.ones((8, WIDTH), BF16)
    for i in range(2):
        rows = prod[:, 8 * i : 8 * i + 8, :].reshape(ROWS, WIDTH)
        hi = rows.astype(BF16)
        rest = rows - hi.astype(F32)
        mid = rest.astype(BF16)
        low = (rest - mid.astype(F32)).astype(BF16)
        total = dot(ones, hi, 1, 1) + dot(ones, mid, 1, 1) + dot(ones, low, 1, 1)
        d_ref[0, i : i + 1, :] = total[:1]


def delta_rows(g, o):
    out = pl.pallas_call(
        delta_kernel,
        grid=(KV // 2,),
        out_shape=jax.ShapeDtypeStruct((KV // 2, 2, ROWS), F32),
        in_specs=[pl.BlockSpec((TOK, 16, WIDTH), lambda i: (0, i, 0))] * 2,
        out_specs=pl.BlockSpec((1, 2, ROWS), lambda i: (i, 0, 0)),
        compiler_params=params(),
        name="delta_rows",
    )(g, o)
    return out.reshape(KV, ROWS)


RANGES = {0: ((0, 128), (0, 256)), 1: ((0, 256), (0, 256)), 2: ((0, 256), (128, 256))}


def main_kernel(parts, where, lens, *refs):
    refs = list(refs)
    q_own, q_sib, g_own, g_sib, st_own, st_sib = refs[:6]
    pos = 6
    kv_in = []
    for _ in parts:
        kv_in.append((refs[pos], refs[pos + 1]))
        pos += 2
    dq_own, dq_sib = refs[pos : pos + 2]
    pos += 2
    dkv_out = []
    for _ in parts:
        dkv_out.append((refs[pos], refs[pos + 1]))
        pos += 2
    q_s, g_s, st_s, kv_s, acc_s, dq_s, lo_s = refs[pos:]
    step = pl.program_id(0)
    index = where[0]
    core = index % 2
    chip = index // 2

    @pl.when(step == 0)
    def _():
        for s in range(2):
            at = (chip * 2 + s) * TOK + lax.shift_right_logical(
                lax.broadcasted_iota(jnp.int32, (1, ROWS), 1), 3
            )
            low = jnp.zeros((1, ROWS), jnp.int32)
            end = jnp.int32(0)
            for n in range(NDOC):
                end = end + lens[n]
                low = jnp.where(at >= end, end, low)
            lo_s[s] = low

    for src, dst in ((q_own, q_s), (g_own, g_s)):
        x = src[...].astype(F32)
        for i in range(2):
            dst[core, i] = x[:, 8 * i : 8 * i + 8, :].reshape(ROWS, WIDTH).astype(BF16)
    for src, dst in ((q_sib, q_s), (g_sib, g_s)):
        x = src[...].astype(F32)
        for i in range(2):
            dst[1 - core, i] = x[:, 8 * i : 8 * i + 8, :].reshape(ROWS, WIDTH).astype(BF16)
    st_s[core] = st_own[...]
    st_s[1 - core] = st_sib[...]
    for n, (same, flip) in enumerate(kv_in):
        kv_s[n, :, :, pl.ds(pl.multiple_of(core * TOK, TOK), TOK), :] = same[...]
        kv_s[n, :, :, pl.ds(pl.multiple_of((1 - core) * TOK, TOK), TOK), :] = flip[...]
    acc_s[...] = jnp.zeros_like(acc_s)

    for i in range(2):
        for s in range(2):
            q = q_s[s, i]
            g = g_s[s, i]
            lse = st_s[s, 0, 0, i : i + 1] * LOG2E
            delta = st_s[s, 1, 0, i : i + 1]
            low = lo_s[s]
            dq = None
            for n, part in enumerate(parts):
                first, last = RANGES[part][s]
                size = last - first
                k = kv_s[n, 0, i, first:last, :]
                v = kv_s[n, 1, i, first:last, :]
                base = (chip - part) * 2 * TOK + first
                j = base + lax.broadcasted_iota(jnp.int32, (size, ROWS), 0)
                visible = j >= low
                if part == 0:
                    at = (chip * 2 + s) * TOK + lax.shift_right_logical(
                        lax.broadcasted_iota(jnp.int32, (1, ROWS), 1), 3
                    )
                    visible = visible & (j <= at)
                score = dot(k, q, 1, 1)
                prob = jnp.where(visible, jnp.exp2(score * (SCALE * LOG2E) - lse), 0.0)
                acc_s[n, 1, i, first:last, :] += dot(prob.astype(BF16), g, 1, 0)
                dprob = dot(v, g, 1, 1)
                ds = (prob * (dprob - delta)).astype(BF16)
                acc_s[n, 0, i, first:last, :] += dot(ds, q, 1, 0) * SCALE
                d = dot(k, ds, 0, 0)
                dq = d if dq is None else dq + d
            dq_s[s, :, i] = (jnp.transpose(dq) * SCALE).reshape(TOK, 8, WIDTH)

    for n, (same, flip) in enumerate(dkv_out):
        same[...] = acc_s[n, :, :, pl.ds(pl.multiple_of(core * TOK, TOK), TOK), :].astype(same.dtype)
        flip[...] = acc_s[n, :, :, pl.ds(pl.multiple_of((1 - core) * TOK, TOK), TOK), :].astype(
            flip.dtype
        )
    dq_own[...] = dq_s[core].reshape(TOK, 16, WIDTH).astype(BF16)
    dq_sib[...] = dq_s[1 - core].reshape(TOK, 16, WIDTH).astype(BF16)


def main_call(parts, where, lens, q_own, q_sib, g_own, g_sib, st_own, st_sib, kvs):
    heads = pl.BlockSpec((TOK, 16, WIDTH), lambda i, w, l: (0, 2 * (w[0] % 2) + i, 0))
    stats = pl.BlockSpec((2, 1, 2, ROWS), lambda i, w, l: (0, 2 * (w[0] % 2) + i, 0, 0))
    kv_spec = pl.BlockSpec((2, 2, TOK, WIDTH), lambda i, w, l: (0, i, 0, 0))
    dq_spec = pl.BlockSpec((TOK, 16, WIDTH), lambda i, w, l: (0, i, 0))
    dq_shape = jax.ShapeDtypeStruct((TOK, HEADS // 2, WIDTH), BF16)
    out_shape = [dq_shape, dq_shape]
    for part in parts:
        out_shape.append(
            jax.ShapeDtypeStruct((2, HALF, TOK, WIDTH), F32 if part == 0 else BF16)
        )
        out_shape.append(jax.ShapeDtypeStruct((2, HALF, TOK, WIDTH), BF16))
    flat = []
    for same, flip in kvs:
        flat += [same.reshape(2, HALF, TOK, WIDTH), flip.reshape(2, HALF, TOK, WIDTH)]
    size = len(parts)
    outs = pl.pallas_call(
        functools.partial(main_kernel, parts),
        grid_spec=pltpu.PrefetchScalarGridSpec(
            num_scalar_prefetch=2,
            grid=(2,),
            in_specs=[heads] * 4 + [stats] * 2 + [kv_spec] * len(flat),
            out_specs=[dq_spec] * 2 + [kv_spec] * len(flat),
            scratch_shapes=[
                pltpu.VMEM((2, 2, ROWS, WIDTH), BF16),
                pltpu.VMEM((2, 2, ROWS, WIDTH), BF16),
                pltpu.VMEM((2, 2, 1, 2, ROWS), F32),
                pltpu.VMEM((size, 2, 2, 2 * TOK, WIDTH), BF16),
                pltpu.VMEM((size, 2, 2, 2 * TOK, WIDTH), F32),
                pltpu.VMEM((2, TOK, 2, 8, WIDTH), F32),
                pltpu.VMEM((2, 1, ROWS), jnp.int32),
            ],
        ),
        out_shape=out_shape,
        compiler_params=params(),
        name="attention_grads",
    )(where, lens, q_own, q_sib, g_own, g_sib, st_own, st_sib, *flat)
    return outs


def final_kernel(where, own, sib, s1, f1, s2, f2, dk_ref, dv_ref, scr):
    core = where[0] % 2
    scr[core] = own[...] + s1[...].astype(F32) + s2[...].astype(F32)
    scr[1 - core] = sib[...].astype(F32) + f1[...].astype(F32) + f2[...].astype(F32)
    for which, out in enumerate((dk_ref, dv_ref)):
        x = jnp.concatenate([scr[0, which], scr[1, which]], axis=0)
        out[...] = jnp.transpose(x, (1, 0, 2)).astype(BF16)


def final_sum(where, *arrays):
    out = jax.ShapeDtypeStruct((TOK, KV, WIDTH), BF16)
    return pl.pallas_call(
        final_kernel,
        out_shape=(out, out),
        in_specs=[pl.BlockSpec(memory_space=pltpu.SMEM)]
        + [pl.BlockSpec(memory_space=pltpu.VMEM)] * 6,
        out_specs=(pl.BlockSpec(memory_space=pltpu.VMEM),) * 2,
        scratch_shapes=[pltpu.VMEM((2, 2, HALF, TOK, WIDTH), F32)],
        compiler_params=params(),
        name="final_sum",
    )(where, *arrays)


def dq_kernel(where, own, sib, out):
    core = where[0] % 2
    mine = (pl.program_id(0) // 2) == core

    @pl.when(mine)
    def _():
        out[...] = own[...]

    @pl.when(jnp.logical_not(mine))
    def _():
        out[...] = sib[...]


def dq_join(where, own, sib):
    def own_map(i, w):
        return (0, i % 2, 0)

    return pl.pallas_call(
        dq_kernel,
        grid_spec=pltpu.PrefetchScalarGridSpec(
            num_scalar_prefetch=1,
            grid=(4,),
            in_specs=[pl.BlockSpec((TOK, 16, WIDTH), own_map)] * 2,
            out_specs=pl.BlockSpec((TOK, 16, WIDTH), lambda i, w: (0, i, 0)),
        ),
        out_shape=jax.ShapeDtypeStruct((TOK, HEADS, WIDTH), BF16),
        compiler_params=params(),
        name="dq_join",
    )(where, own, sib)


def move(x, count, chips, flip):
    pairs = []
    for i in range(count):
        chip, core = divmod(i, 2)
        pairs.append((i, ((chip + chips) % (count // 2)) * 2 + (core ^ flip)))
    return lax.ppermute(x, "ctx", pairs)


def per_device(queries, keys, values, output, output_cotangent, logsumexp_rows, doc_lengths):
    count = lax.axis_size("ctx")
    index = lax.axis_index("ctx").astype(jnp.int32)
    where = index[None]
    shift = functools.partial(move, count=count)

    same, flip = kv_prep(where, keys, values)
    same1 = shift(same, chips=1, flip=0)
    flip1 = shift(flip, chips=1, flip=1)
    same2 = shift(same, chips=2, flip=0)
    flip2 = shift(flip, chips=2, flip=1)
    flip0 = shift(flip, chips=0, flip=1)
    q_sib = shift(queries, chips=0, flip=1)
    g_sib = shift(output_cotangent, chips=0, flip=1)
    delta = delta_rows(output_cotangent, output)
    lse = logsumexp_rows.reshape(TOK, KV, HEADS // KV).transpose(1, 0, 2).reshape(KV, ROWS)
    st_own = jnp.stack([lse, delta]).reshape(2, KV // 2, 2, ROWS)
    st_sib = shift(st_own, chips=0, flip=1)

    outs = main_call(
        (0, 1, 2),
        where,
        doc_lengths,
        queries,
        q_sib,
        output_cotangent,
        g_sib,
        st_own,
        st_sib,
        [(same, flip0), (same1, flip1), (same2, flip2)],
    )
    dq_own, dq_sib, d0s, d0f, d1s, d1f, d2s, d2f = outs
    r1s = shift(d1s, chips=-1, flip=0)
    r1f = shift(d1f, chips=-1, flip=1)
    r2s = shift(d2s, chips=-2, flip=0)
    r2f = shift(d2f, chips=-2, flip=1)
    r0 = shift(d0f, chips=0, flip=1)
    dq_got = shift(dq_sib, chips=0, flip=1)
    query_grad = dq_join(where, dq_own, dq_got)
    key_grad, value_grad = final_sum(where, d0s, r0, r1s, r1f, r2s, r2f)
    return (query_grad, key_grad, value_grad)


def solution(mesh):
    rows = P(("dp", "ctx"), None, None)
    return jax.shard_map(
        per_device,
        mesh=mesh,
        in_specs=(rows,) * 5 + (P(("dp", "ctx"), None), P("dp")),
        out_specs=(rows,) * 3,
        check_vma=False,
    )
```

```python
import functools

import jax
import jax.numpy as jnp
from jax import lax
from jax.experimental import pallas as pl
from jax.experimental.pallas import tpu as pltpu
from jax.sharding import PartitionSpec as P

TOK = 128
WIDTH = 128
HEADS = 64
KV = 8
HALF = KV // 2
ROWS = TOK * (HEADS // KV)
NDOC = 16
SCALE = WIDTH ** (-0.5)
LOG2E = 1.4426950408889634
F32 = jnp.float32
BF16 = jnp.bfloat16
VMEM_LIMIT = 48 * 1024 * 1024
PACK_VMEM = 62 * 1024 * 1024
PART_VMEM = (VMEM_LIMIT, VMEM_LIMIT, VMEM_LIMIT)


def params(limit=VMEM_LIMIT):
    return pltpu.CompilerParams(vmem_limit_bytes=limit)


def dot(a, b, ca, cb):
    return lax.dot_general(a, b, (((ca,), (cb,)), ((), ())), preferred_element_type=F32)


PACK = 2 * ROWS + 2 * TOK + 48


def split3(x):
    hi = x.astype(BF16)
    rest = x - hi.astype(F32)
    mid = rest.astype(BF16)
    low = (rest - mid.astype(F32)).astype(BF16)
    return hi, mid, low


def fold(row):
    return jnp.concatenate([row[:, c * WIDTH : (c + 1) * WIDTH] for c in range(8)], axis=0)


def unfold(block):
    return jnp.concatenate([block[c : c + 1] for c in range(8)], axis=1)


def spread_lse(lse_ref, lse_s):
    row = lax.broadcasted_iota(jnp.int32, (TOK, ROWS), 1)
    tok = lax.broadcasted_iota(jnp.int32, (TOK, ROWS), 0)
    spread = jnp.where(lax.shift_right_logical(row, 3) == tok, 1.0, 0.0).astype(BF16)
    head = lax.broadcasted_iota(jnp.int32, (8, ROWS), 0)
    pick = head == (lax.broadcasted_iota(jnp.int32, (8, ROWS), 1) & 7)
    for n, term in enumerate(split3(lse_ref[...])):
        full = dot(term, spread, 1, 0)
        for h in range(KV):
            rows = jnp.where(pick, full[8 * h : 8 * h + 8], 0.0)
            lse_s[h, n : n + 1] = jnp.sum(rows, axis=0, keepdims=True)


def row_sums(x):
    hi = x.astype(BF16)
    mid = (x - hi.astype(F32)).astype(BF16)
    ones = jnp.ones((2 * WIDTH, WIDTH), BF16)
    total = dot(jnp.concatenate([hi, mid], axis=1), ones, 1, 0)
    eye = lax.broadcasted_iota(jnp.int32, (WIDTH, WIDTH), 0) == lax.broadcasted_iota(
        jnp.int32, (WIDTH, WIDTH), 1
    )
    rows = []
    for c in range(8):
        block = jnp.where(eye, total[c * WIDTH : (c + 1) * WIDTH], 0.0)
        rows.append(jnp.sum(block, axis=0, keepdims=True))
    return jnp.concatenate(rows, axis=0)


def emit_pack(out, q_ref, g_ref, o_ref, lse_s, half, kv):
    step = pl.program_id(0)
    q = q_ref[...].astype(F32)
    g = g_ref[...].astype(F32)
    prod = g * o_ref[...].astype(F32)
    for i in range(2):
        heads = slice(8 * i, 8 * i + 8)
        out[i, :ROWS] = q[:, heads, :].reshape(ROWS, WIDTH).astype(BF16)
        out[i, ROWS : 2 * ROWS] = g[:, heads, :].reshape(ROWS, WIDTH).astype(BF16)
        out[i, 2 * ROWS : 2 * ROWS + TOK] = kv(0, i)
        out[i, 2 * ROWS + TOK : 2 * ROWS + 2 * TOK] = kv(1, i)
        delta = split3(row_sums(prod[:, heads, :].reshape(ROWS, WIDTH)))
        lse = lse_s[half * HALF + 2 * step + i]
        rows = [fold(lse[n : n + 1]) for n in range(3)] + [t.astype(F32) for t in delta]
        out[i, 2 * ROWS + 2 * TOK :] = jnp.concatenate(rows, axis=0).astype(BF16)


def sib_kernel(where, q, g, o, lse_ref, k_ref, v_ref, out, same_ref, flip_ref, lse_s, kv_s):
    step = pl.program_id(0)
    core = where[0] % 2

    @pl.when(step == 0)
    def _():
        for n, ref in enumerate((k_ref, v_ref)):
            x = jnp.transpose(ref[...].astype(F32), (1, 0, 2)).astype(BF16)
            kv_s[0, n] = x[:HALF]
            kv_s[1, n] = x[HALF:]
        same_ref[...] = kv_s[core]
        flip_ref[...] = kv_s[1 - core]
        spread_lse(lse_ref, lse_s)

    emit_pack(out, q, g, o, lse_s, 1 - core, lambda n, i: kv_s[1 - core, n, 2 * step + i])


def own_kernel(where, q, g, o, lse_ref, same_ref, out, lse_s):
    @pl.when(pl.program_id(0) == 0)
    def _():
        spread_lse(lse_ref, lse_s)

    emit_pack(out, q, g, o, lse_s, where[0] % 2, lambda n, i: same_ref[n, i])


def pack_call(kernel, flip, where, args, in_specs, out_shape, out_specs, scratch, name):
    def heads(i, w):
        core = w[0] % 2
        return (0, 2 * (1 - core if flip else core) + i, 0)

    raw = pl.BlockSpec((TOK, 16, WIDTH), heads)
    pack_shape = jax.ShapeDtypeStruct((HALF, PACK, WIDTH), BF16)
    return pl.pallas_call(
        kernel,
        grid_spec=pltpu.PrefetchScalarGridSpec(
            num_scalar_prefetch=1,
            grid=(2,),
            in_specs=[raw, raw, raw, pl.BlockSpec((HEADS, TOK), lambda i, w: (0, 0))] + in_specs,
            out_specs=[pl.BlockSpec((2, PACK, WIDTH), lambda i, w: (i, 0, 0))] + out_specs,
            scratch_shapes=[pltpu.VMEM((KV, 3, ROWS), F32)] + scratch,
        ),
        out_shape=[pack_shape] + out_shape,
        compiler_params=params(PACK_VMEM),
        name=name,
    )(where, *args)


def pack_sib(where, q, g, o, lse, k, v):
    full = pl.BlockSpec((TOK, KV, WIDTH), lambda i, w: (0, 0, 0))
    kv = pl.BlockSpec((2, HALF, TOK, WIDTH), lambda i, w: (0, 0, 0, 0))
    shape = jax.ShapeDtypeStruct((2, HALF, TOK, WIDTH), BF16)
    scratch = [pltpu.VMEM((2, 2, HALF, TOK, WIDTH), BF16)]
    args = (q, g, o, lse, k, v)
    return pack_call(
        sib_kernel, True, where, args, [full] * 2, [shape] * 2, [kv] * 2, scratch, "pack_sib"
    )


def pack_own(where, q, g, o, lse, same):
    kv = pl.BlockSpec((2, 2, TOK, WIDTH), lambda i, w: (0, i, 0, 0))
    args = (q, g, o, lse, same)
    return pack_call(own_kernel, False, where, args, [kv], [], [], [], "pack_own")[0]


RANGES = {0: ((0, 128), (0, 256)), 1: ((0, 256), (0, 256)), 2: ((0, 256), (128, 256))}
CHUNK = 1024


def positions(chip, s):
    at = lax.shift_right_logical(lax.broadcasted_iota(jnp.int32, (1, ROWS), 1), 3)
    return at + (chip * 2 + s) * TOK


def doc_starts(lens, at):
    low = jnp.zeros((1, ROWS), jnp.int32)
    end = jnp.int32(0)
    for n in range(NDOC):
        end = end + lens[n]
        low = jnp.where(at >= end, end, low)
    return low


def grads(part, chip, s, k, v, q, g, lse, delta, low, first, emit_dq):
    size = k.shape[0]
    base = (chip - part) * 2 * TOK + first
    dk = dv = None
    at = positions(chip, s) if part == 0 else None
    for r in range(0, ROWS, CHUNK):
        cols = slice(r, r + CHUNK)
        qc = q[cols]
        gc = g[cols]
        j = base + lax.broadcasted_iota(jnp.int32, (size, CHUNK), 0)
        visible = j >= low[:, cols]
        if part == 0:
            visible = visible & (j <= at[:, cols])
        score = dot(k, qc, 1, 1)
        prob = jnp.where(visible, jnp.exp2(score * (SCALE * LOG2E) - lse[:, cols]), 0.0)
        dvc = dot(prob.astype(BF16), gc, 1, 0)
        dprob = dot(v, gc, 1, 1)
        ds = (prob * (dprob - delta[:, cols])).astype(BF16)
        dkc = dot(ds, qc, 1, 0)
        dk = dkc if dk is None else dk + dkc
        dv = dvc if dv is None else dv + dvc
        emit_dq(cols, dot(k, ds, 0, 0))
    return dk * SCALE, dv


def phase_kernel(part, heads, where, lens, *refs):
    own, sib = refs[:2]
    qg_s, st_s, kv_s, acc_s, dq_s = refs[-5:]
    index = where[0]
    core = index % 2
    chip = index // 2
    own_at = pl.ds(pl.multiple_of(core * TOK, TOK), TOK)
    sib_at = pl.ds(pl.multiple_of((1 - core) * TOK, TOK), TOK)
    for half, src in ((core, own), (1 - core, sib)):
        qg_s[half] = src[:, : 2 * ROWS, :]
        for i in range(heads):
            st = src[i, 2 * ROWS + 2 * TOK :, :].astype(F32)
            st_s[half, i, 0:1] = unfold(st[0:8] + st[8:16] + st[16:24]) * LOG2E
            st_s[half, i, 1:2] = unfold(st[24:32] + st[32:40] + st[40:48])
    if part == 0:
        dq_out, d_same, d_flip = refs[2:5]
        for half, src in ((own_at, own), (sib_at, sib)):
            kv_s[0, :, half, :] = src[:, 2 * ROWS : 2 * ROWS + TOK, :]
            kv_s[1, :, half, :] = src[:, 2 * ROWS + TOK : 2 * ROWS + 2 * TOK, :]
    else:
        same, flip, dq_in = refs[2:5]
        kv_s[:, :, own_at, :] = same[...]
        kv_s[:, :, sib_at, :] = flip[...]
        if part == 1:
            dq_out, d_same, d_flip = refs[5:8]
        else:
            dq_own, *back, d_same, d_flip = refs[5:12]
    if part != 1:
        acc_s[...] = jnp.zeros_like(acc_s)

    for s in range(2):
        low = doc_starts(lens, positions(chip, s))
        for i in range(heads):
            first, last = RANGES[part][s]

            def emit(cols, d):
                if part == 0:
                    dq_out[s, i, :, cols] = d
                elif part == 1:
                    dq_out[s, i, :, cols] = dq_in[s, i, :, cols] + d
                else:
                    full = jnp.transpose(dq_in[s, i, :, cols] + d) * SCALE
                    dq_s[s, i, cols, :] = full.astype(BF16)

            dk, dv = grads(
                part,
                chip,
                s,
                kv_s[0, i, first:last, :],
                kv_s[1, i, first:last, :],
                qg_s[s, i, :ROWS],
                qg_s[s, i, ROWS:],
                st_s[s, i, 0:1],
                st_s[s, i, 1:2],
                low,
                first,
                emit,
            )
            fresh = part == 1 and s == 0
            acc_s[0, i, first:last, :] = dk if fresh else acc_s[0, i, first:last, :] + dk
            acc_s[1, i, first:last, :] = dv if fresh else acc_s[1, i, first:last, :] + dv

    d_same[...] = acc_s[:, :, own_at, :].astype(d_same.dtype)
    d_flip[...] = acc_s[:, :, sib_at, :].astype(d_flip.dtype)
    if part == 2:
        dq_own[...] = dq_s[core]
        for n in range(HALF // heads):

            @pl.when(pl.program_id(0) == n)
            def _():
                for i in range(heads):
                    back[n * heads + i][...] = dq_s[1 - core, i]


def phase(part, where, lens, own, sib, same=None, flip=None, dq=None, heads=2):
    pack_spec = pl.BlockSpec((heads, PACK, WIDTH), lambda i, w, l: (i, 0, 0))
    kv_spec = pl.BlockSpec((2, heads, TOK, WIDTH), lambda i, w, l: (0, i, 0, 0))
    dq_spec = pl.BlockSpec((2, heads, WIDTH, ROWS), lambda i, w, l: (0, i, 0, 0))
    dq_shape = jax.ShapeDtypeStruct((2, HALF, WIDTH, ROWS), F32)
    kv_shape = jax.ShapeDtypeStruct((2, HALF, TOK, WIDTH), BF16)
    args = [own, sib]
    in_specs = [pack_spec, pack_spec]
    if part == 0:
        out_shape = [dq_shape, jax.ShapeDtypeStruct((2, HALF, TOK, WIDTH), F32), kv_shape]
        out_specs = [dq_spec, kv_spec, kv_spec]
    else:
        args += [same, flip, dq]
        in_specs += [kv_spec, kv_spec, dq_spec]
        if part == 1:
            out_shape = [dq_shape, kv_shape, kv_shape]
            out_specs = [dq_spec, kv_spec, kv_spec]
        else:
            out_shape = [
                jax.ShapeDtypeStruct((HALF, ROWS, WIDTH), BF16),
                *[jax.ShapeDtypeStruct((ROWS, WIDTH), BF16)] * HALF,
                kv_shape,
                kv_shape,
            ]
            out_specs = [
                pl.BlockSpec((heads, ROWS, WIDTH), lambda i, w, l: (i, 0, 0)),
                *[pl.BlockSpec((ROWS, WIDTH), lambda i, w, l: (0, 0))] * HALF,
                kv_spec,
                kv_spec,
            ]
    return pl.pallas_call(
        functools.partial(phase_kernel, part, heads),
        grid_spec=pltpu.PrefetchScalarGridSpec(
            num_scalar_prefetch=2,
            grid=(HALF // heads,),
            in_specs=in_specs,
            out_specs=out_specs,
            scratch_shapes=[
                pltpu.VMEM((2, heads, 2 * ROWS, WIDTH), BF16),
                pltpu.VMEM((2, heads, 2, ROWS), F32),
                pltpu.VMEM((2, heads, 2 * TOK, WIDTH), BF16),
                pltpu.VMEM((2, heads, 2 * TOK, WIDTH), F32),
                pltpu.VMEM((2, heads, ROWS, WIDTH), BF16),
            ],
        ),
        out_shape=out_shape,
        compiler_params=params(PART_VMEM[part]),
        name=f"grads_part{part}",
    )(where, lens, *args)


def near_kernel(own, s1, f1, r0, out):
    out[0] = own[...] + s1[...].astype(F32)
    out[1] = f1[...].astype(F32) + r0[...].astype(F32)


def near_sum(own, s1, f1, r0):
    spec = pl.BlockSpec((1, HALF, TOK, WIDTH), lambda i: (i, 0, 0, 0))
    return pl.pallas_call(
        near_kernel,
        grid=(2,),
        out_shape=jax.ShapeDtypeStruct((2, 2, HALF, TOK, WIDTH), F32),
        in_specs=[spec] * 4,
        out_specs=pl.BlockSpec((2, 1, HALF, TOK, WIDTH), lambda i: (0, i, 0, 0, 0)),
        compiler_params=params(),
        name="near_sum",
    )(own, s1, f1, r0)


def final_kernel(where, near, s2, f2, dk_ref, dv_ref, scr):
    core = where[0] % 2
    for which, out in enumerate((dk_ref, dv_ref)):
        scr[core] = near[0, which] + s2[which].astype(F32)
        scr[1 - core] = near[1, which] + f2[which].astype(F32)
        x = jnp.concatenate([scr[0], scr[1]], axis=0)
        out[...] = jnp.transpose(x, (1, 0, 2)).astype(BF16)


def final_sum(where, near, s2, f2):
    out = jax.ShapeDtypeStruct((TOK, KV, WIDTH), BF16)
    kv = pl.BlockSpec((2, HALF, TOK, WIDTH), lambda i, w: (0, 0, 0, 0))
    full = pl.BlockSpec((TOK, KV, WIDTH), lambda i, w: (0, 0, 0))
    return pl.pallas_call(
        final_kernel,
        grid_spec=pltpu.PrefetchScalarGridSpec(
            num_scalar_prefetch=1,
            grid=(1,),
            in_specs=[
                pl.BlockSpec((2, 2, HALF, TOK, WIDTH), lambda i, w: (0, 0, 0, 0, 0)),
                kv,
                kv,
            ],
            out_specs=[full, full],
            scratch_shapes=[pltpu.VMEM((2, HALF, TOK, WIDTH), F32)],
        ),
        out_shape=(out, out),
        compiler_params=params(),
        name="final_sum",
    )(where, near, s2, f2)


def join_kernel(where, own, b0, b1, b2, b3, out):
    step = pl.program_id(0)
    mine = (step // 2) == where[0] % 2

    def emit(x0, x1):
        x = [x.astype(F32).reshape(TOK, 8, WIDTH) for x in (x0, x1)]
        out[...] = jnp.concatenate(x, axis=1).astype(BF16)

    @pl.when(mine)
    def _():
        emit(own[0], own[1])

    @pl.when(jnp.logical_not(mine) & (step % 2 == 0))
    def _():
        emit(b0[...], b1[...])

    @pl.when(jnp.logical_not(mine) & (step % 2 == 1))
    def _():
        emit(b2[...], b3[...])


def dq_join(where, own, back):
    return pl.pallas_call(
        join_kernel,
        grid_spec=pltpu.PrefetchScalarGridSpec(
            num_scalar_prefetch=1,
            grid=(4,),
            in_specs=[pl.BlockSpec((2, ROWS, WIDTH), lambda i, w: (i % 2, 0, 0))]
            + [pl.BlockSpec((ROWS, WIDTH), lambda i, w: (0, 0))] * HALF,
            out_specs=pl.BlockSpec((TOK, 16, WIDTH), lambda i, w: (0, i, 0)),
        ),
        out_shape=jax.ShapeDtypeStruct((TOK, HEADS, WIDTH), BF16),
        compiler_params=params(),
        name="dq_join",
    )(where, own, *back)


def move(x, count, chips, flip):
    pairs = []
    for i in range(count):
        chip, core = divmod(i, 2)
        pairs.append((i, ((chip + chips) % (count // 2)) * 2 + (core ^ flip)))
    return lax.ppermute(x, "ctx", pairs)


def per_device(queries, keys, values, output, output_cotangent, logsumexp_rows, doc_lengths):
    count = lax.axis_size("ctx")
    where = lax.axis_index("ctx").astype(jnp.int32)[None]
    shift = functools.partial(move, count=count)

    lse = logsumexp_rows.T
    to_sib, same, flip = pack_sib(
        where, queries, output_cotangent, output, lse, keys, values
    )
    sib = shift(to_sib, chips=0, flip=1)
    same1 = shift(same, chips=1, flip=0)
    flip1 = shift(flip, chips=1, flip=1)
    same2 = shift(same, chips=2, flip=0)
    flip2 = shift(flip, chips=2, flip=1)
    own = pack_own(where, queries, output_cotangent, output, lse, same)

    dq, d0s, d0f = phase(0, where, doc_lengths, own, sib)
    r0 = shift(d0f, chips=0, flip=1)
    dq, d1s, d1f = phase(1, where, doc_lengths, own, sib, same1, flip1, dq)
    r1s = shift(d1s, chips=-1, flip=0)
    r1f = shift(d1f, chips=-1, flip=1)
    dq_own, *to_back, d2s, d2f = phase(2, where, doc_lengths, own, sib, same2, flip2, dq)
    d2s, r1s = lax.optimization_barrier((d2s, r1s))
    d2f, r1f = lax.optimization_barrier((d2f, r1f))
    r2s = shift(d2s, chips=-2, flip=0)
    r2f = shift(d2f, chips=-2, flip=1)
    back = [shift(x, chips=0, flip=1) for x in to_back]
    near = near_sum(d0s, r1s, r1f, r0)
    query_grad = dq_join(where, dq_own, back)
    key_grad, value_grad = final_sum(where, near, r2s, r2f)
    return (query_grad, key_grad, value_grad)


def solution(mesh):
    rows = P(("dp", "ctx"), None, None)
    return jax.shard_map(
        per_device,
        mesh=mesh,
        in_specs=(rows,) * 5 + (P(("dp", "ctx"), None), P("dp")),
        out_specs=(rows,) * 3,
        check_vma=False,
    )
```

```python
import functools

import jax
import jax.numpy as jnp
from jax import lax
from jax.experimental import pallas as pl
from jax.experimental.pallas import tpu as pltpu
from jax.sharding import PartitionSpec as P

TOK = 128
WIDTH = 128
HEADS = 64
KV = 8
HALF = KV // 2
ROWS = TOK * (HEADS // KV)
NDOC = 16
SCALE = WIDTH ** (-0.5)
LOG2E = 1.4426950408889634
F32 = jnp.float32
BF16 = jnp.bfloat16
VMEM_LIMIT = 48 * 1024 * 1024
PACK_VMEM = 62 * 1024 * 1024
PART_VMEM = (36 * 1024 * 1024,) * 3


def params(limit=VMEM_LIMIT):
    return pltpu.CompilerParams(vmem_limit_bytes=limit)


def dot(a, b, ca, cb):
    return lax.dot_general(a, b, (((ca,), (cb,)), ((), ())), preferred_element_type=F32)


PACK = 2 * ROWS + 2 * TOK + 48


def split3(x):
    hi = x.astype(BF16)
    rest = x - hi.astype(F32)
    mid = rest.astype(BF16)
    low = (rest - mid.astype(F32)).astype(BF16)
    return hi, mid, low


def fold(row):
    return jnp.concatenate([row[:, c * WIDTH : (c + 1) * WIDTH] for c in range(8)], axis=0)


def unfold(block):
    return jnp.concatenate([block[c : c + 1] for c in range(8)], axis=1)


def spread_lse(lse_ref, lse_s):
    row = lax.broadcasted_iota(jnp.int32, (TOK, ROWS), 1)
    tok = lax.broadcasted_iota(jnp.int32, (TOK, ROWS), 0)
    spread = jnp.where(lax.shift_right_logical(row, 3) == tok, 1.0, 0.0).astype(BF16)
    head = lax.broadcasted_iota(jnp.int32, (8, ROWS), 0)
    pick = head == (lax.broadcasted_iota(jnp.int32, (8, ROWS), 1) & 7)
    for n, term in enumerate(split3(lse_ref[...])):
        full = dot(term, spread, 1, 0)
        for h in range(KV):
            rows = jnp.where(pick, full[8 * h : 8 * h + 8], 0.0)
            lse_s[h, n : n + 1] = jnp.sum(rows, axis=0, keepdims=True)


def row_sums(x):
    hi = x.astype(BF16)
    mid = (x - hi.astype(F32)).astype(BF16)
    ones = jnp.ones((2 * WIDTH, WIDTH), BF16)
    total = dot(jnp.concatenate([hi, mid], axis=1), ones, 1, 0)
    eye = lax.broadcasted_iota(jnp.int32, (WIDTH, WIDTH), 0) == lax.broadcasted_iota(
        jnp.int32, (WIDTH, WIDTH), 1
    )
    rows = []
    for c in range(8):
        block = jnp.where(eye, total[c * WIDTH : (c + 1) * WIDTH], 0.0)
        rows.append(jnp.sum(block, axis=0, keepdims=True))
    return jnp.concatenate(rows, axis=0)


def emit_pack(out, q_ref, g_ref, o_ref, lse_s, half, kv):
    step = pl.program_id(0)
    q = q_ref[...].astype(F32)
    g = g_ref[...].astype(F32)
    prod = g * o_ref[...].astype(F32)
    for i in range(2):
        heads = slice(8 * i, 8 * i + 8)
        out[i, :ROWS] = q[:, heads, :].reshape(ROWS, WIDTH).astype(BF16)
        out[i, ROWS : 2 * ROWS] = g[:, heads, :].reshape(ROWS, WIDTH).astype(BF16)
        out[i, 2 * ROWS : 2 * ROWS + TOK] = kv(0, i)
        out[i, 2 * ROWS + TOK : 2 * ROWS + 2 * TOK] = kv(1, i)
        delta = split3(row_sums(prod[:, heads, :].reshape(ROWS, WIDTH)))
        lse = lse_s[half * HALF + 2 * step + i]
        rows = [fold(lse[n : n + 1]) for n in range(3)] + [t.astype(F32) for t in delta]
        out[i, 2 * ROWS + 2 * TOK :] = jnp.concatenate(rows, axis=0).astype(BF16)


def sib_kernel(where, q, g, o, lse_ref, k_ref, v_ref, out, same_ref, flip_ref, lse_s, kv_s):
    step = pl.program_id(0)
    core = where[0] % 2

    @pl.when(step == 0)
    def _():
        for n, ref in enumerate((k_ref, v_ref)):
            x = jnp.transpose(ref[...].astype(F32), (1, 0, 2)).astype(BF16)
            kv_s[0, n] = x[:HALF]
            kv_s[1, n] = x[HALF:]
        same_ref[...] = kv_s[core]
        flip_ref[...] = kv_s[1 - core]
        spread_lse(lse_ref, lse_s)

    emit_pack(out, q, g, o, lse_s, 1 - core, lambda n, i: kv_s[1 - core, n, 2 * step + i])


def own_kernel(where, q, g, o, lse_ref, same_ref, out, lse_s):
    @pl.when(pl.program_id(0) == 0)
    def _():
        spread_lse(lse_ref, lse_s)

    emit_pack(out, q, g, o, lse_s, where[0] % 2, lambda n, i: same_ref[n, i])


def pack_call(kernel, flip, where, args, in_specs, out_shape, out_specs, scratch, name):
    def heads(i, w):
        core = w[0] % 2
        return (0, 2 * (1 - core if flip else core) + i, 0)

    raw = pl.BlockSpec((TOK, 16, WIDTH), heads)
    pack_shape = jax.ShapeDtypeStruct((HALF, PACK, WIDTH), BF16)
    return pl.pallas_call(
        kernel,
        grid_spec=pltpu.PrefetchScalarGridSpec(
            num_scalar_prefetch=1,
            grid=(2,),
            in_specs=[raw, raw, raw, pl.BlockSpec((HEADS, TOK), lambda i, w: (0, 0))] + in_specs,
            out_specs=[pl.BlockSpec((2, PACK, WIDTH), lambda i, w: (i, 0, 0))] + out_specs,
            scratch_shapes=[pltpu.VMEM((KV, 3, ROWS), F32)] + scratch,
        ),
        out_shape=[pack_shape] + out_shape,
        compiler_params=params(PACK_VMEM),
        name=name,
    )(where, *args)


def pack_sib(where, q, g, o, lse, k, v):
    full = pl.BlockSpec((TOK, KV, WIDTH), lambda i, w: (0, 0, 0))
    kv = pl.BlockSpec((2, HALF, TOK, WIDTH), lambda i, w: (0, 0, 0, 0))
    shape = jax.ShapeDtypeStruct((2, HALF, TOK, WIDTH), BF16)
    scratch = [pltpu.VMEM((2, 2, HALF, TOK, WIDTH), BF16)]
    args = (q, g, o, lse, k, v)
    return pack_call(
        sib_kernel, True, where, args, [full] * 2, [shape] * 2, [kv] * 2, scratch, "pack_sib"
    )


def pack_own(where, q, g, o, lse, same):
    kv = pl.BlockSpec((2, 2, TOK, WIDTH), lambda i, w: (0, i, 0, 0))
    args = (q, g, o, lse, same)
    return pack_call(own_kernel, False, where, args, [kv], [], [], [], "pack_own")[0]


RANGES = {0: ((0, 128), (0, 256)), 1: ((0, 256), (0, 256)), 2: ((0, 256), (128, 256))}


def positions(chip, s):
    at = lax.shift_right_logical(lax.broadcasted_iota(jnp.int32, (1, ROWS), 1), 3)
    return at + (chip * 2 + s) * TOK


def doc_starts(lens, at):
    low = jnp.zeros((1, ROWS), jnp.int32)
    end = jnp.int32(0)
    for n in range(NDOC):
        end = end + lens[n]
        low = jnp.where(at >= end, end, low)
    return low


def products(k, v, q, g):
    return dot(k, q, 1, 1), dot(v, g, 1, 1)


def weights(part, chip, s, first, score, dprob, lse, delta, low):
    base = (chip - part) * 2 * TOK + first
    j = base + lax.broadcasted_iota(jnp.int32, score.shape, 0)
    visible = j >= low
    if part == 0:
        visible = visible & (j <= positions(chip, s))
    prob = jnp.where(visible, jnp.exp2(score * (SCALE * LOG2E) - lse), 0.0)
    return prob.astype(BF16), (prob * (dprob - delta)).astype(BF16)


def phase_kernel(part, where, lens, *refs):
    index = where[0]
    core = index % 2
    chip = index // 2
    own_at = pl.ds(pl.multiple_of(core * TOK, TOK), TOK)
    sib_at = pl.ds(pl.multiple_of((1 - core) * TOK, TOK), TOK)
    copies = []
    if part == 0:
        own, sib, rows_s, dq_out, d_same, d_flip, st_s, acc_s, dq_s, sems = refs
        for i in range(HALF):
            for n, (half, src) in enumerate(((core, own), (1 - core, sib))):
                copy = pltpu.make_async_copy(src.at[i], rows_s.at[half, i], sems.at[n, i])
                copy.start()
                copies.append(copy)
    elif part == 1:
        rows_s, dq_in, same, flip, dq_out, d_same, d_flip, st_s, kv_s, acc_s, dq_s = refs
    else:
        rows_s, dq_in, same, flip, dq_own, *back = refs[:9]
        d_same, d_flip, st_s, kv_s, acc_s, dq_s = refs[9:]
    if part != 0:
        kv_s[:, :, own_at, :] = same[...]
        kv_s[:, :, sib_at, :] = flip[...]

    def stats(i, s):
        st = rows_s[s, i, 2 * ROWS + 2 * TOK :, :].astype(F32)
        st_s[s, i, 0:1] = unfold(st[0:8] + st[8:16] + st[16:24]) * LOG2E
        st_s[s, i, 1:2] = unfold(st[24:32] + st[32:40] + st[40:48])

    if part != 1:
        acc_s[...] = jnp.zeros_like(acc_s)
    lows = [doc_starts(lens, positions(chip, s)) for s in range(2)]
    items = [(i, s) for i in range(HALF) for s in range(2)]

    def key_rows(which, i, s):
        first, last = RANGES[part][s]
        if part != 0:
            return kv_s[which, i, first:last, :]
        at = slice(2 * ROWS + which * TOK, 2 * ROWS + (which + 1) * TOK)
        if s == 0:
            return rows_s[0, i, at, :]
        return jnp.concatenate([rows_s[0, i, at, :], rows_s[1, i, at, :]], axis=0)

    def start(i, s):
        if part == 0 and s == 0:
            for copy in copies[2 * i : 2 * i + 2]:
                copy.wait()
        stats(i, s)
        return products(
            key_rows(0, i, s), key_rows(1, i, s), rows_s[s, i, :ROWS], rows_s[s, i, ROWS : 2 * ROWS]
        )

    ahead = start(*items[0])
    for n, (i, s) in enumerate(items):
        first, last = RANGES[part][s]
        score, dprob = ahead
        if n + 1 < len(items):
            ahead = start(*items[n + 1])
        prob, ds = weights(
            part, chip, s, first, score, dprob, st_s[s, i, 0:1], st_s[s, i, 1:2], lows[s]
        )
        dv = dot(prob, rows_s[s, i, ROWS : 2 * ROWS], 1, 0)
        dk = dot(ds, rows_s[s, i, :ROWS], 1, 0) * SCALE
        fresh = part == 1 and s == 0
        acc_s[0, i, first:last, :] = dk if fresh else acc_s[0, i, first:last, :] + dk
        acc_s[1, i, first:last, :] = dv if fresh else acc_s[1, i, first:last, :] + dv
        d = dot(key_rows(0, i, s), ds, 0, 0)
        if part == 0:
            dq_out[s, i] = d
        elif part == 1:
            dq_out[s, i] = dq_in[s, i] + d
        else:
            dq_s[s, i] = (jnp.transpose(dq_in[s, i] + d) * SCALE).astype(BF16)

    d_same[...] = acc_s[:, :, own_at, :].astype(d_same.dtype)
    d_flip[...] = acc_s[:, :, sib_at, :].astype(d_flip.dtype)
    if part == 2:
        dq_own[...] = dq_s[core]
        for i in range(HALF):
            back[i][...] = dq_s[1 - core, i]


def phase(part, where, lens, rows, same=None, flip=None, dq=None):
    vmem = pl.BlockSpec(memory_space=pltpu.VMEM)
    hbm = pl.BlockSpec(memory_space=pltpu.HBM)
    kv_spec = pl.BlockSpec((2, HALF, TOK, WIDTH), lambda i, w, l: (0, 0, 0, 0))
    rows_shape = jax.ShapeDtypeStruct((2, HALF, PACK, WIDTH), BF16)
    dq_shape = jax.ShapeDtypeStruct((2, HALF, WIDTH, ROWS), F32)
    kv_shape = jax.ShapeDtypeStruct((2, HALF, TOK, WIDTH), BF16)
    scratch = [pltpu.VMEM((2, HALF, 2, ROWS), F32)]
    if part != 0:
        scratch.append(pltpu.VMEM((2, HALF, 2 * TOK, WIDTH), BF16))
    scratch += [
        pltpu.VMEM((2, HALF, 2 * TOK, WIDTH), F32),
        pltpu.VMEM((2, HALF, ROWS, WIDTH) if part == 2 else (8, WIDTH), BF16),
    ]
    if part == 0:
        args = rows
        in_specs = [hbm, hbm]
        out_shape = [rows_shape, dq_shape, jax.ShapeDtypeStruct((2, HALF, TOK, WIDTH), F32), kv_shape]
        out_specs = [vmem, vmem, kv_spec, kv_spec]
        scratch.append(pltpu.SemaphoreType.DMA((2, HALF)))
    else:
        args = (rows, dq, same, flip)
        in_specs = [vmem, vmem, kv_spec, kv_spec]
        if part == 1:
            out_shape = [dq_shape, kv_shape, kv_shape]
            out_specs = [vmem, kv_spec, kv_spec]
        else:
            out_shape = [
                jax.ShapeDtypeStruct((HALF, ROWS, WIDTH), BF16),
                *[jax.ShapeDtypeStruct((ROWS, WIDTH), BF16)] * HALF,
                kv_shape,
                kv_shape,
            ]
            out_specs = [
                pl.BlockSpec((HALF, ROWS, WIDTH), lambda i, w, l: (0, 0, 0)),
                *[pl.BlockSpec((ROWS, WIDTH), lambda i, w, l: (0, 0))] * HALF,
                kv_spec,
                kv_spec,
            ]
    return pl.pallas_call(
        functools.partial(phase_kernel, part),
        grid_spec=pltpu.PrefetchScalarGridSpec(
            num_scalar_prefetch=2,
            grid=(1,),
            in_specs=in_specs,
            out_specs=out_specs,
            scratch_shapes=scratch,
        ),
        out_shape=out_shape,
        compiler_params=params(PART_VMEM[part]),
        name=f"grads_part{part}",
    )(where, lens, *args)


def near_kernel(own, s1, f1, r0, out):
    out[0] = own[...] + s1[...].astype(F32)
    out[1] = f1[...].astype(F32) + r0[...].astype(F32)


def near_sum(own, s1, f1, r0):
    spec = pl.BlockSpec((1, HALF, TOK, WIDTH), lambda i: (i, 0, 0, 0))
    return pl.pallas_call(
        near_kernel,
        grid=(2,),
        out_shape=jax.ShapeDtypeStruct((2, 2, HALF, TOK, WIDTH), F32),
        in_specs=[spec] * 4,
        out_specs=pl.BlockSpec((2, 1, HALF, TOK, WIDTH), lambda i: (0, i, 0, 0, 0)),
        compiler_params=params(),
        name="near_sum",
    )(own, s1, f1, r0)


def final_kernel(where, near, s2, f2, dk_ref, dv_ref, scr):
    core = where[0] % 2
    for which, out in enumerate((dk_ref, dv_ref)):
        scr[core] = near[0, which] + s2[which].astype(F32)
        scr[1 - core] = near[1, which] + f2[which].astype(F32)
        x = jnp.concatenate([scr[0], scr[1]], axis=0)
        out[...] = jnp.transpose(x, (1, 0, 2)).astype(BF16)


def final_sum(where, near, s2, f2):
    out = jax.ShapeDtypeStruct((TOK, KV, WIDTH), BF16)
    kv = pl.BlockSpec((2, HALF, TOK, WIDTH), lambda i, w: (0, 0, 0, 0))
    full = pl.BlockSpec((TOK, KV, WIDTH), lambda i, w: (0, 0, 0))
    return pl.pallas_call(
        final_kernel,
        grid_spec=pltpu.PrefetchScalarGridSpec(
            num_scalar_prefetch=1,
            grid=(1,),
            in_specs=[
                pl.BlockSpec((2, 2, HALF, TOK, WIDTH), lambda i, w: (0, 0, 0, 0, 0)),
                kv,
                kv,
            ],
            out_specs=[full, full],
            scratch_shapes=[pltpu.VMEM((2, HALF, TOK, WIDTH), F32)],
        ),
        out_shape=(out, out),
        compiler_params=params(),
        name="final_sum",
    )(where, near, s2, f2)


def join_kernel(where, own, b0, b1, b2, b3, out):
    step = pl.program_id(0)
    mine = (step // 2) == where[0] % 2

    def emit(x0, x1):
        x = [x.astype(F32).reshape(TOK, 8, WIDTH) for x in (x0, x1)]
        out[...] = jnp.concatenate(x, axis=1).astype(BF16)

    @pl.when(mine)
    def _():
        emit(own[0], own[1])

    @pl.when(jnp.logical_not(mine) & (step % 2 == 0))
    def _():
        emit(b0[...], b1[...])

    @pl.when(jnp.logical_not(mine) & (step % 2 == 1))
    def _():
        emit(b2[...], b3[...])


def dq_join(where, own, back):
    return pl.pallas_call(
        join_kernel,
        grid_spec=pltpu.PrefetchScalarGridSpec(
            num_scalar_prefetch=1,
            grid=(4,),
            in_specs=[pl.BlockSpec((2, ROWS, WIDTH), lambda i, w: (i % 2, 0, 0))]
            + [pl.BlockSpec((ROWS, WIDTH), lambda i, w: (0, 0))] * HALF,
            out_specs=pl.BlockSpec((TOK, 16, WIDTH), lambda i, w: (0, i, 0)),
        ),
        out_shape=jax.ShapeDtypeStruct((TOK, HEADS, WIDTH), BF16),
        compiler_params=params(),
        name="dq_join",
    )(where, own, *back)


def move(x, count, chips, flip):
    pairs = []
    for i in range(count):
        chip, core = divmod(i, 2)
        pairs.append((i, ((chip + chips) % (count // 2)) * 2 + (core ^ flip)))
    return lax.ppermute(x, "ctx", pairs)


def per_device(queries, keys, values, output, output_cotangent, logsumexp_rows, doc_lengths):
    count = lax.axis_size("ctx")
    where = lax.axis_index("ctx").astype(jnp.int32)[None]
    shift = functools.partial(move, count=count)

    lse = logsumexp_rows.T
    to_sib, same, flip = pack_sib(
        where, queries, output_cotangent, output, lse, keys, values
    )
    sib = shift(to_sib, chips=0, flip=1)
    same1 = shift(same, chips=1, flip=0)
    flip1 = shift(flip, chips=1, flip=1)
    own = pack_own(where, queries, output_cotangent, output, lse, same)

    far_same, far_flip, own = lax.optimization_barrier((same, flip, own))
    same2 = shift(far_same, chips=2, flip=0)
    flip2 = shift(far_flip, chips=2, flip=1)
    rows, dq, d0s, d0f = phase(0, where, doc_lengths, (own, sib))
    r0 = shift(d0f, chips=0, flip=1)
    dq, d1s, d1f = phase(1, where, doc_lengths, rows, same1, flip1, dq)
    r1s = shift(d1s, chips=-1, flip=0)
    r1f = shift(d1f, chips=-1, flip=1)
    dq, r0 = lax.optimization_barrier((dq, r0))
    dq_own, *to_back, d2s, d2f = phase(2, where, doc_lengths, rows, same2, flip2, dq)
    to_back[2], r1s = lax.optimization_barrier((to_back[2], r1s))
    to_back[3], r1f = lax.optimization_barrier((to_back[3], r1f))
    r2s = shift(d2s, chips=-2, flip=0)
    r2f = shift(d2f, chips=-2, flip=1)
    back = [shift(x, chips=0, flip=1) for x in to_back]
    near = near_sum(d0s, r1s, r1f, r0)
    query_grad = dq_join(where, dq_own, back)
    key_grad, value_grad = final_sum(where, near, r2s, r2f)
    return (query_grad, key_grad, value_grad)


def solution(mesh):
    rows = P(("dp", "ctx"), None, None)
    return jax.shard_map(
        per_device,
        mesh=mesh,
        in_specs=(rows,) * 5 + (P(("dp", "ctx"), None), P("dp")),
        out_specs=(rows,) * 3,
        check_vma=False,
    )
```
